128 devices in a mesh: wide: 16 (over z, y_hi, core), narrow: 8 (over y_lo, x).
Axes of the slice: x: 4, y: 4 (y_hi: 2, y_lo: 2; y = y_hi * 2 + y_lo), z: 4, core: 2. Of those that a mesh axis runs over, the one named last changes fastest.
Arguments:
- residual_in: bfloat16 [512, 18432], P('wide', 'narrow'), may hold values from -80 to 80
- query: bfloat16 [512, 12288], P('narrow', 'wide'), may hold values from -12 to 12
- cache: bfloat16 [8, 64, 1536, 512], P('narrow', 'wide'), may hold values from -200 to 200
- lengths: int32 [8, 64], P('narrow', 'wide'), may hold values from 2 to 1536, as said below
- gate_weight: bfloat16 [18432, 18432], P('narrow', 'wide'), may hold values from -0.046875 to 0.046875
- up_weight: bfloat16 [18432, 18432], P('narrow', 'wide'), may hold values from -0.046875 to 0.046875
- down_weight: bfloat16 [18432, 18432], P('wide', 'narrow'), may hold values from -0.046875 to 0.046875
- out_weight: bfloat16 [12288, 18432], P('wide', 'narrow'), may hold values from -0.21875 to 0.21875
Outputs:
- update: bfloat16 [512, 18432], P('wide', 'narrow')
The draws below stay inside these ranges and needn't reach their ends.
Inputs may be any that keep to these rules, and one draw needn't show every extreme that they name: `lengths`: some row's length is exactly 1536.
All inputs are finite; a program needn't handle non-finite values.
Results may differ from the reference program's by a relative error of at most 0.0062.
Values may be sent and summed in bfloat16 or wider, within the bound.
A program may use at most 128 MiB of HBM per device.

```python
import math
import jax
import jax.numpy as jnp
from jax import lax

D = 18432
HEADS = 48
HEAD = 256
FF = 18432
CACHE = 1536
QCOLS = 12288
KV = 512
SLAB_ROWS = 64
ROWS = 512


def query_base(key):
    normal_part = jnp.clip(jax.random.normal(key, (ROWS, QCOLS), jnp.float32), -5.9, 5.9)
    return normal_part


def draw_query(key, part):
    base = query_base(key)
    return base.astype(jnp.bfloat16)


def draw_cache(key, part):
    key = jax.random.fold_in(key, 11)
    first_key = jax.random.fold_in(key, 0)
    entries = jnp.clip(jax.random.normal(first_key, (ROWS, CACHE, KV), jnp.float32), -6.0, 6.0)
    return entries.reshape(ROWS // SLAB_ROWS, SLAB_ROWS, CACHE, KV).astype(jnp.bfloat16)


def draw_lengths(key, part):
    key = jax.random.fold_in(key, 23)
    first_key, second_key = jax.random.split(key, 2)
    drawn = jax.random.randint(first_key, (ROWS,), 2, CACHE + 1)
    longest = jax.random.randint(second_key, (), 0, ROWS)
    drawn = jnp.where(jnp.arange(ROWS) == longest, CACHE, drawn)
    return drawn.reshape(ROWS // SLAB_ROWS, SLAB_ROWS).astype(jnp.int32)


def draw_residual_in(key, part):
    key = jax.random.fold_in(key, 31)
    first_key, second_key = jax.random.split(key, 2)
    position = jnp.arange(D).astype(jnp.float32) / D
    entries = jnp.clip(jax.random.normal(first_key, (ROWS, D), jnp.float32), -6.0, 6.0)
    column_scale = jnp.exp(2.302585 * position)
    row_scale = jnp.exp(2.302585 * jax.random.uniform(second_key, (ROWS, 1), jnp.float32, 0.0, 1.0))
    return (0.1 * entries * row_scale * column_scale[None, :]).astype(jnp.bfloat16)


def level_of(rng, shape, pieces, least, top_value):
    loudness = 1.0
    for dim, parts in pieces:
        draws = jax.random.uniform(jax.random.fold_in(jax.random.fold_in(rng, 6), dim), (parts,), jnp.float32, least / len(pieces), top_value / len(pieces))
        loudness = loudness * jnp.repeat(jnp.exp(draws), shape[dim] // parts).reshape((-1,) + (1,) * (len(shape) - 1 - dim))
    return loudness


def bell_draw(own_key, extent, scale, most, pieces=(), held_as=jnp.bfloat16):
    factor_of = level_of(own_key, extent, pieces, -0.22, 0.18) if pieces else 1.0
    values = jax.random.normal(own_key, extent, jnp.float32) * scale * factor_of
    return jnp.minimum(jnp.maximum(values, -most), most).astype(held_as)


def setup_inputs(seed: int = 0) -> dict:
    splits = jax.random.split(jax.random.key(seed), 9)
    residual_in = draw_residual_in(jax.random.fold_in(splits[8], 71), 0)
    query = draw_query(jax.random.fold_in(splits[8], 71), 0)
    cache = draw_cache(jax.random.fold_in(splits[8], 71), 0)
    lengths = draw_lengths(jax.random.fold_in(splits[8], 71), 0)
    gate_weight = bell_draw(splits[4], (D, FF), D ** -0.5, 0.046875, ((0, 8), (1, 16)))
    up_weight = bell_draw(splits[5], (D, FF), D ** -0.5, 0.046875, ((0, 8), (1, 16)))
    down_weight = bell_draw(splits[6], (FF, D), FF ** -0.5, 0.046875, ((0, 16), (1, 8)))
    out_weight = bell_draw(splits[7], (QCOLS, D), (QCOLS // 16) ** -0.5, 0.21875, ((0, 16), (1, 8)))
    return {"residual_in": residual_in, "query": query, "cache": cache, "lengths": lengths, "gate_weight": gate_weight, "up_weight": up_weight, "down_weight": down_weight, "out_weight": out_weight}


def reference(residual_in, query, cache, lengths, gate_weight, up_weight, down_weight, out_weight):
    rows_f = residual_in.astype(jnp.float32)
    mean = lax.optimization_barrier(jnp.mean(rows_f, axis=1, keepdims=True))
    variance = lax.optimization_barrier(jnp.mean(rows_f * rows_f, axis=1, keepdims=True)) - mean * mean
    normed = ((rows_f - mean) * lax.rsqrt(variance + 1e-06)).astype(jnp.bfloat16)
    gate = jnp.dot(normed, gate_weight, preferred_element_type=jnp.float32)
    up_proj = jnp.dot(normed, up_weight, preferred_element_type=jnp.float32)
    hidden = (jax.nn.silu(gate) * up_proj).astype(jnp.bfloat16)
    ffn_part = jnp.dot(hidden, down_weight, preferred_element_type=jnp.float32)
    flat_cache = cache.reshape(ROWS, CACHE, KV)
    flat_lengths = lengths.reshape(ROWS)

    def one_row(items):
        query_row, cache_row, length = items
        query_heads = query_row.reshape(HEADS, HEAD)
        keys = cache_row[:, :HEAD]
        values = cache_row[:, HEAD:]
        scores = jnp.dot(query_heads, keys.T, preferred_element_type=jnp.float32) / math.sqrt(HEAD)
        valid = jnp.arange(CACHE) < length
        scores = jnp.where(valid[None, :], scores, -jnp.inf)
        top = lax.optimization_barrier(jnp.max(scores, axis=1, keepdims=True))
        weights = jnp.exp(scores - top)
        probs = (weights / lax.optimization_barrier(jnp.sum(weights, axis=1, keepdims=True))).astype(jnp.bfloat16)
        return jnp.dot(probs, values, preferred_element_type=jnp.float32).astype(jnp.bfloat16).reshape(QCOLS)
    context = lax.map(one_row, (query, flat_cache, flat_lengths))
    attn_part = jnp.dot(context, out_weight, preferred_element_type=jnp.float32)
    return (ffn_part + attn_part).astype(jnp.bfloat16)
```

```python
import jax
import jax.numpy as jnp
from jax import lax
from jax.experimental import pallas as pl
from jax.experimental.pallas import tpu as pltpu
from jax.sharding import PartitionSpec as P

HEADS = 48
HEAD = 256
MESH = pl.DeviceIdType.MESH
BF = jnp.bfloat16
F32 = jnp.float32
STEPS = (0, 1, 3, 2)


def dot(a, b):
    return jnp.dot(a, b, preferred_element_type=F32)


def pick(rows, cols, rule):
    i = lax.broadcasted_iota(jnp.int32, (rows, cols), 0)
    k = lax.broadcasted_iota(jnp.int32, (rows, cols), 1)
    return jnp.where(rule(i, k), 1.0, 0.0).astype(BF)


def kernel(
    res, query, lengths, cache_hbm, wg_hbm, wu_hbm, wd_hbm, wo_hbm, out,
    wgu, wd, wo, cache, xg, st, pb, rb, hid, ctxg, acc, cs, rc, se, rz, own, ys, ry,
    qs, qr, qh, cb, csd, crv, lsem, ssem, rsem,
):
    w = lax.axis_index("wide")
    n = lax.axis_index("narrow")
    z, yh, c = w // 4, (w // 2) % 2, w % 2
    yl, x = n // 4, n % 4
    width = res.shape[1] * 8
    half = wg_hbm.shape[1]
    taken = [0]

    def near(k):
        return ((yl + k // 4) % 2) * 4 + (x + k % 4) % 4

    def far(k):
        return ((z + k // 4) % 4) * 4 + ((yh + (k // 2) % 2) % 2) * 2 + (c + k % 2) % 2

    def send(src, dst, wt, nt):
        i = taken[0]
        taken[0] += 1
        copy = pltpu.make_async_remote_copy(
            src_ref=src, dst_ref=dst, send_sem=ssem.at[i], recv_sem=rsem.at[i],
            device_id=(wt, nt), device_id_type=MESH,
        )
        copy.start()
        return copy

    pw = z * 4 + (1 - yh) * 2 + c
    sw = z * 4 + yh * 2 + (1 - c)
    sent = []

    loads = []
    for i, (src, dst) in enumerate((
        (cache_hbm.at[0], cache),
        (wg_hbm, wgu.at[:, pl.ds(0, half)]),
        (wu_hbm, wgu.at[:, pl.ds(half, half)]),
        (wo_hbm, wo),
        (wd_hbm, wd),
    )):
        copy = pltpu.make_async_copy(src, dst, lsem.at[i])
        copy.start()
        loads.append(copy)

    barrier = pltpu.get_barrier_semaphore()
    for k in range(1, 8):
        pl.semaphore_signal(barrier, inc=1, device_id=(w, near(k)), device_id_type=MESH)
    for k in range(1, 16):
        pl.semaphore_signal(barrier, inc=1, device_id=(far(k), n), device_id_type=MESH)

    rows_f = res[...].astype(F32)
    total = jnp.sum(rows_f, axis=1, keepdims=True)
    square = jnp.sum(rows_f * rows_f, axis=1, keepdims=True)
    lane = lax.broadcasted_iota(jnp.int32, (32, 128), 1)
    mine = jnp.where(lane < 64, total, square)
    st[0] = mine
    moved = jnp.zeros((256, HEAD), F32)
    for h in range(3):
        table = pick(256, 64, lambda i, k: ((i >> 4) == (k >> 2)) & ((i & 15) == 4 * h + (k & 3)))
        moved += dot(table, query[:, h * HEAD:(h + 1) * HEAD])
    qs[...] = moved.astype(BF).reshape(16, 16, HEAD)
    pl.semaphore_wait(barrier, 22)

    stats = [send(st.at[0], st.at[k], w, near(k)) for k in range(1, 8)]
    queries = [send(qs.at[far(k)], qr.at[w], far(k), n) for k in range(1, 16)]
    qr[w] = qs[w]
    sent += stats + queries
    for k, copy in enumerate(stats):
        copy.wait_recv()
        mine += st[k + 1]
    mean = mine[:, 0:1] / width
    variance = mine[:, 64:65] / width - mean * mean
    xg[z, yh, c] = ((rows_f - mean) * lax.rsqrt(variance + 1e-06)).astype(BF)

    def rows_at(zz, yy):
        return xg.at[zz, yy, c]

    def z_at(d):
        return ((z + d) % 4) * 4 + yh * 2 + c

    mate = send(rows_at(z, yh), rows_at(z, yh), pw, n)
    sib = send(rows_at(z, yh), rows_at(z, yh), sw, n)
    first = {d: send(rows_at(z, yh), rows_at(z, yh), z_at(d), n) for d in (1, 3)}
    sent += [mate, sib, first[1], first[3]]

    for copy in queries:
        copy.wait_recv()
    table = pick(192, 256, lambda i, k: (i == (k & 3) * 48 + (k >> 4) * 3 + ((k >> 2) & 3)) & (((k >> 2) & 3) < 3))
    qh[...] = dot(table, qr[...].reshape(256, HEAD)).astype(BF)
    loads[0].wait()

    def attend(r):
        scores = lax.dot_general(
            qh[r * 48:(r + 1) * 48, :], cache[r, :, 0:HEAD], (((1,), (1,)), ((), ())),
            preferred_element_type=F32,
        ) * (1.0 / 16.0)
        spot = lax.broadcasted_iota(jnp.int32, scores.shape, 1)
        scores = jnp.where(spot < lengths[0, r], scores, -jnp.inf)
        top = jnp.max(scores, axis=1, keepdims=True)
        weights = jnp.exp(scores - top)
        probs = (weights / jnp.sum(weights, axis=1, keepdims=True)).astype(BF)
        cb[r * 48:(r + 1) * 48, :] = dot(probs, cache[r, :, HEAD:2 * HEAD]).astype(BF)

    attend(0)

    mate.wait_recv()
    psib = send(rows_at(z, 1 - yh), rows_at(z, 1 - yh), sw, n)
    second = {d: send(rows_at(z, 1 - yh), rows_at(z, 1 - yh), z_at(d), n) for d in (1, 3)}
    first[2] = send(rows_at(z, yh), rows_at(z, yh), z_at(2), n)
    second[2] = send(rows_at(z, 1 - yh), rows_at(z, 1 - yh), z_at(2), n)
    sent += [psib, *second.values(), first[2]]
    attend(1)

    passed = {}

    def hand_over(d):
        first[d].wait_recv()
        second[d].wait_recv()
        zc = (z + 4 - d) % 4
        passed[d] = send(xg.at[zc, :, c], xg.at[zc, :, c], sw, n)
        sent.append(passed[d])

    parts, hidden_parts, cores, zs = {}, {}, {}, {}

    def first_product(j):
        d = STEPS[j]
        zc = (z + 4 - d) % 4
        if d == 0:
            sib.wait_recv()
            psib.wait_recv()
            loads[1].wait()
            loads[2].wait()
        else:
            passed[d].wait_recv()
        rows = xg[zc].reshape(128, xg.shape[4])

        def tile(t, carry):
            cols = pl.ds(pl.multiple_of(t * 256, 256), 256)
            pb[j, :, :, cols] = dot(rows, wgu[:, cols]).astype(BF).reshape(8, 16, 256)
            return carry

        lax.fori_loop(0, wgu.shape[1] // 256, tile, 0)
        parts[j] = [send(pb.at[j, near(k)], rb.at[j, k], w, near(k)) for k in range(1, 8)]
        sent.extend(parts[j])

    def hidden_piece(j):
        summed = pb[j, n].astype(F32)
        for k in range(1, 8):
            parts[j][k - 1].wait_recv()
            summed += rb[j, k].astype(F32)
        gate, up = summed[:, :half], summed[:, half:]
        hid[j, n] = (gate / (1.0 + jnp.exp(-gate)) * up).astype(BF)
        hidden_parts[j] = [send(hid.at[j, n], hid.at[j, n], w, near(k)) for k in range(1, 8)]
        sent.extend(hidden_parts[j])

    def second_product(j):
        zc = (z + 4 - STEPS[j]) % 4
        for copy in hidden_parts[j]:
            copy.wait_recv()
        if j == 0:
            for copy in contexts:
                copy.wait_recv()
            loads[3].wait()
            loads[4].wait()
        rows = hid[j].reshape(128, half)
        heads = ctxg[pl.ds(2 * zc, 2)].reshape(128, ctxg.shape[2])
        slot = j % 2

        def tile(t, carry):
            cols = pl.ds(pl.multiple_of(t * 256, 256), 256)
            value = dot(rows, wd[:, cols]) + dot(heads, wo[:, cols])
            acc[slot, :, :, :, cols] = value.reshape(2, 2, 32, 256)
            return carry

        lax.fori_loop(0, wd.shape[1] // 256, tile, 0)
        cs[j] = acc[slot, :, 1 - c].astype(BF)
        cores[j] = send(cs.at[j], rc.at[j], sw, n)
        sent.append(cores[j])

    def core_sum(j):
        d = STEPS[j]
        cores[j].wait_recv()
        value = acc[j % 2, :, c] + rc[j].astype(F32)
        if d == 0:
            own[...] = value
        else:
            se[j] = value.astype(BF)
            e = 4 - d
            zs[e] = send(se.at[j], rz.at[e], z_at(e), n)
            sent.append(zs[e])

    first_product(0)
    hand_over(1)
    hand_over(3)
    attend(2)
    first_product(1)
    attend(3)
    table = pick(256, 192, lambda k, i: (i == (k & 3) * 48 + (k >> 4) * 3 + ((k >> 2) & 3)) & (((k >> 2) & 3) < 3))
    csd[...] = dot(table, cb[...]).astype(BF).reshape(16, 16, HEAD)
    turned = [send(csd.at[far(k)], crv.at[w], far(k), n) for k in range(1, 16)]
    crv[w] = csd[w]
    sent += turned
    hand_over(2)
    first_product(2)
    hidden_piece(0)
    first_product(3)
    for copy in turned:
        copy.wait_recv()
    arrived = crv[...].reshape(256, HEAD)
    for h in range(3):
        table = pick(64, 256, lambda i, k: ((k >> 4) == (i >> 2)) & ((k & 15) == 4 * h + (i & 3)))
        ctxg[n, :, h * HEAD:(h + 1) * HEAD] = dot(table, arrived).astype(BF)
    contexts = [send(ctxg.at[n], ctxg.at[n], w, near(k)) for k in range(1, 8)]
    sent += contexts
    hidden_piece(1)
    second_product(0)
    hidden_piece(2)
    core_sum(0)
    second_product(1)
    hidden_piece(3)
    core_sum(1)
    second_product(2)
    core_sum(2)
    second_product(3)
    core_sum(3)

    def finished(b):
        value = own[b]
        for e in (3, 1, 2):
            value += rz[e, b].astype(F32)
        return value

    for e in (3, 1, 2):
        zs[e].wait_recv()
    ys[...] = finished(1 - yh).astype(BF)
    last = send(ys, ry, pw, n)
    sent.append(last)
    value = finished(yh)
    for copy in sent:
        copy.wait_send()
    last.wait_recv()
    out[...] = (value + ry[...].astype(F32)).astype(BF)


def local(residual_in, query, cache, lengths, gate_weight, up_weight, down_weight, out_weight):
    rows, width = residual_in.shape
    half = gate_weight.shape[1]
    cols = query.shape[1]
    places = cache.shape[2]
    vmem = pl.BlockSpec(memory_space=pltpu.VMEM)
    hbm = pl.BlockSpec(memory_space=pl.ANY)
    copies = 160
    return pl.pallas_call(
        kernel,
        out_shape=jax.ShapeDtypeStruct((rows, width), BF),
        in_specs=[vmem, vmem, pl.BlockSpec(memory_space=pltpu.SMEM), hbm, hbm, hbm, hbm, hbm],
        out_specs=vmem,
        scratch_shapes=[
            pltpu.VMEM((width, 2 * half), BF),
            pltpu.VMEM((half, width), BF),
            pltpu.VMEM((cols, width), BF),
            pltpu.VMEM((4, places, 2 * HEAD), BF),
            pltpu.VMEM((4, 2, 2, 32, width), BF),
            pltpu.VMEM((8, 32, 128), F32),
            pltpu.VMEM((4, 8, 16, 2 * half), BF),
            pltpu.VMEM((4, 8, 16, 2 * half), BF),
            pltpu.VMEM((4, 8, 16, half), BF),
            pltpu.VMEM((8, 64, cols), BF),
            pltpu.VMEM((2, 2, 2, 32, width), F32),
            pltpu.VMEM((4, 2, 32, width), BF),
            pltpu.VMEM((4, 2, 32, width), BF),
            pltpu.VMEM((4, 2, 32, width), BF),
            pltpu.VMEM((4, 2, 32, width), BF),
            pltpu.VMEM((2, 32, width), F32),
            pltpu.VMEM((32, width), BF),
            pltpu.VMEM((32, width), BF),
            pltpu.VMEM((16, 16, HEAD), BF),
            pltpu.VMEM((16, 16, HEAD), BF),
            pltpu.VMEM((192, HEAD), BF),
            pltpu.VMEM((192, HEAD), BF),
            pltpu.VMEM((16, 16, HEAD), BF),
            pltpu.VMEM((16, 16, HEAD), BF),
            pltpu.SemaphoreType.DMA((5,)),
            pltpu.SemaphoreType.DMA((copies,)),
            pltpu.SemaphoreType.DMA((copies,)),
        ],
        compiler_params=pltpu.CompilerParams(
            collective_id=0, has_side_effects=True, vmem_limit_bytes=58 << 20
        ),
        name="layer",
    )(residual_in, query, lengths, cache, gate_weight, up_weight, down_weight, out_weight)


def solution(mesh):
    return jax.shard_map(
        local,
        mesh=mesh,
        in_specs=(
            P("wide", "narrow"),
            P("narrow", "wide"),
            P("narrow", "wide", None, None),
            P("narrow", "wide"),
            P("narrow", "wide"),
            P("narrow", "wide"),
            P("wide", "narrow"),
            P("wide", "narrow"),
        ),
        out_specs=P("wide", "narrow"),
        check_vma=False,
    )
```

```python
import jax
import jax.numpy as jnp
from jax import lax
from jax.experimental import pallas as pl
from jax.experimental.pallas import tpu as pltpu
from jax.sharding import PartitionSpec as P

HEADS = 48
HEAD = 256
MESH = pl.DeviceIdType.MESH
BF = jnp.bfloat16
F32 = jnp.float32
STEPS = (1, 3, 2, 0)
DIMS = "aby"
ORDERS = ("aby", "bya", "yab")
WIDE = "abhc"
TURNS = "chab"


def whole(p):
    return 4 * (2 * ((p >> 2) & 1) + ((p >> 3) ^ ((p >> 2) & 1))) + (p & 3)


def dot(a, b):
    return jnp.dot(a, b, preferred_element_type=F32)


def pick(rows, cols, rule):
    i = lax.broadcasted_iota(jnp.int32, (rows, cols), 0)
    k = lax.broadcasted_iota(jnp.int32, (rows, cols), 1)
    return jnp.where(rule(i, k), 1.0, 0.0).astype(BF)


def kernel(
    res, query, lengths, cache_hbm, wg_hbm, wu_hbm, wd_hbm, wo_hbm, out,
    wgu, wd, wo, cache, xg, xn, st, sg, pb, r1, t2, r2, t3, r3, hid, ctxg, acc, cs, rc, sy, ry, ysum, se, rz,
    qs, qv, qh, cb, csd, crv, lsem, ssem, rsem,
):
    w = lax.axis_index("wide")
    n = lax.axis_index("narrow")
    z, yh, c = w // 4, (w // 2) % 2, w % 2
    yl, x = n // 4, n % 4
    width = res.shape[1] * 8
    half = wg_hbm.shape[1]
    third = half // 3
    wide_tile = 256
    taken = [0]
    pending = []

    place = {"a": ((x + 1) % 4) // 2, "b": x // 2, "y": yl}
    across = {"a": yl * 4 + x + 1 - 2 * (x % 2), "b": yl * 4 + 3 - x, "y": (1 - yl) * 4 + x}

    pw = z * 4 + (1 - yh) * 2 + c
    sw = z * 4 + yh * 2 + (1 - c)
    wplace = {"a": ((z + 1) % 4) // 2, "b": z // 2, "h": yh, "c": c}
    wacross = {"a": (z + 1 - 2 * (z % 2)) * 4 + yh * 2 + c, "b": (3 - z) * 4 + yh * 2 + c, "h": pw, "c": sw}

    def spot(lead, dims, fixed):
        return tuple(lead) + tuple(fixed.get(d, slice(None)) for d in dims)

    def near(k):
        return ((yl + k // 4) % 2) * 4 + (x + k % 4) % 4

    def z_at(d):
        return ((z + d) % 4) * 4 + yh * 2 + c

    def send(src, dst, wt, nt):
        i = taken[0]
        taken[0] += 1
        copy = pltpu.make_async_remote_copy(
            src_ref=src, dst_ref=dst, send_sem=ssem.at[i], recv_sem=rsem.at[i],
            device_id=(wt, nt), device_id_type=MESH,
        )
        copy.start()
        pending.append(copy)
        return copy

    def drain():
        for copy in pending:
            copy.wait_send()
        pending.clear()

    loads = []

    landed = set()

    def load(src, dst):
        copy = pltpu.make_async_copy(src, dst, lsem.at[len(loads)])
        copy.start()
        loads.append(copy)

    def land(copies):
        for copy in copies:
            if id(copy) not in landed:
                landed.add(id(copy))
                copy.wait()

    for g in range(3):
        load(wg_hbm.at[:, pl.ds(g * third, third)], wgu.at[:, pl.ds(2 * g * third, third)])
        load(wu_hbm.at[:, pl.ds(g * third, third)], wgu.at[:, pl.ds((2 * g + 1) * third, third)])

    barrier = pltpu.get_barrier_semaphore()
    for k in range(1, 8):
        pl.semaphore_signal(barrier, inc=1, device_id=(w, near(k)), device_id_type=MESH)
    for peer in (sw, pw, z_at(1), z_at(3), z_at(2)):
        pl.semaphore_signal(barrier, inc=1, device_id=(peer, n), device_id_type=MESH)

    rows_f = res[...].astype(F32)
    total = jnp.sum(rows_f, axis=1, keepdims=True)
    square = jnp.sum(rows_f * rows_f, axis=1, keepdims=True)
    lane = lax.broadcasted_iota(jnp.int32, (32, 128), 1)
    mine = jnp.where(lane < 64, total, square)
    st[0] = mine
    moved = jnp.zeros((256, HEAD), F32)
    for h in range(3):
        table = pick(256, 64, lambda i, k: (whole(i >> 4) == (k >> 2)) & ((i & 15) == 4 * h + (k & 3)))
        moved += dot(table, query[:, h * HEAD:(h + 1) * HEAD])
    qs[...] = moved.astype(BF).reshape(2, 2, 2, 2, 16, HEAD)
    pl.semaphore_wait(barrier, 12)

    turns = {}

    def turn(held, landing, step):
        if step > 0:
            turns[step - 1].wait_recv()
            turns[step - 1].wait_send()
            pending[:] = [copy for copy in pending if copy is not turns[step - 1]]
            d = TURNS[step - 1]
            held[spot((), WIDE, {d: 1 - wplace[d]})] = landing[step - 1]
        if step < 4:
            d = TURNS[step]
            turns[step] = send(held.at[spot((), WIDE, {d: 1 - wplace[d]})], landing.at[step], wacross[d], n)

    stats = [send(st.at[0], st.at[k], w, near(k)) for k in range(1, 8)]
    xg[z, yh, c] = res[...]

    def rows_at(zz, yy):
        return xg.at[zz, yy, c]

    mate = send(rows_at(z, yh), rows_at(z, yh), pw, n)
    first = {d: send(rows_at(z, yh), rows_at(z, yh), z_at(d), n) for d in (1, 3)}
    sib = [send(rows_at(z, yh), rows_at(z, yh), sw, n)]
    second, passed, gathers = {}, {}, {}
    turn(qs, qv, 0)
    load(cache_hbm.at[0], cache)

    def gather(step):
        if step > 0:
            gathers[step - 1].wait_recv()
        if step < 4:
            d = TURNS[step]
            region = sg.at[spot((), WIDE, {e: wplace[e] for e in TURNS[step:]})]
            gathers[step] = send(region, region, wacross[d], n)

    def statistics():
        sums = mine
        for k, copy in enumerate(stats):
            copy.wait_recv()
            sums += st[k + 1]
        mean = sums[:, 0:1] / width
        variance = sums[:, 64:65] / width - mean * mean
        scale = lax.rsqrt(variance + 1e-06)
        row = lax.broadcasted_iota(jnp.int32, (32, 128), 0)
        line = jnp.sum(
            jnp.where(lane == row, mean, 0.0) + jnp.where(lane == row + 32, scale, 0.0), axis=0, keepdims=True
        )
        sg[wplace["a"], wplace["b"], yh, c] = jnp.broadcast_to(line, (8, 128))
        gather(0)

    def normalize(zc):
        row = lax.broadcasted_iota(jnp.int32, (32, 128), 0)
        for h in range(2):
            for k in range(2):
                line = sg[((zc + 1) % 4) // 2, zc // 2, h, k][0:1, :]
                mean = jnp.sum(jnp.where(lane == row, line, 0.0), axis=1, keepdims=True)
                scale = jnp.sum(jnp.where(lane == row + 32, line, 0.0), axis=1, keepdims=True)
                at = (2 * h + k) * 32
                xn[at:at + 32, :] = ((xg[zc, h, k].astype(F32) - mean) * scale).astype(BF)

    def mates():
        mate.wait_recv()
        for d in (1, 3):
            second[d] = send(rows_at(z, 1 - yh), rows_at(z, 1 - yh), z_at(d), n)
        sib.append(send(rows_at(z, 1 - yh), rows_at(z, 1 - yh), sw, n))
        load(wo_hbm, wo)
        load(wd_hbm, wd)

    def onward(d):
        zc = (z + 4 - d) % 4
        first[d].wait_recv()
        if d == 1:
            first[2] = send(rows_at(zc, yh), rows_at(zc, yh), z_at(1), n)
        second[d].wait_recv()
        if d == 3:
            second[2] = send(rows_at(zc, 1 - yh), rows_at(zc, 1 - yh), z_at(3), n)
        passed[d] = send(xg.at[zc, :, c], xg.at[zc, :, c], sw, n)

    def queries_in():
        table = pick(
            192, 256,
            lambda i, k: (i == (k & 3) * 48 + whole(k >> 4) * 3 + ((k >> 2) & 3)) & (((k >> 2) & 3) < 3),
        )
        qh[...] = dot(table, qs[...].reshape(256, HEAD)).astype(BF)
        land(loads[6:7])

    def attend(r):
        scores = lax.dot_general(
            qh[r * 48:(r + 1) * 48, :], cache[r, :, 0:HEAD], (((1,), (1,)), ((), ())),
            preferred_element_type=F32,
        ) * (1.0 / 16.0)
        at = lax.broadcasted_iota(jnp.int32, scores.shape, 1)
        scores = jnp.where(at < lengths[0, r], scores, -jnp.inf)
        top = jnp.max(scores, axis=1, keepdims=True)
        weights = jnp.exp(scores - top)
        probs = (weights / jnp.sum(weights, axis=1, keepdims=True)).astype(BF)
        cb[r * 48:(r + 1) * 48, :] = dot(probs, cache[r, :, HEAD:2 * HEAD]).astype(BF)

    contexts = {}

    def context_out():
        table = pick(
            256, 192,
            lambda k, i: (i == (k & 3) * 48 + whole(k >> 4) * 3 + ((k >> 2) & 3)) & (((k >> 2) & 3) < 3),
        )
        csd[...] = dot(table, cb[...]).astype(BF).reshape(2, 2, 2, 2, 16, HEAD)
        turn(csd, crv, 0)

    def spread(ref, lead, order, step):
        fixed = {d: place[d] for d in order[:3 - step]}
        region = ref.at[spot(lead, DIMS, fixed)]
        return send(region, region, w, across[order[2 - step]])

    def context_in():
        arrived = csd[...].reshape(256, HEAD)
        for h in range(3):
            table = pick(64, 256, lambda i, k: (whole(k >> 4) == (i >> 2)) & ((k & 15) == 4 * h + (i & 3)))
            ctxg[h, place["a"], place["b"], place["y"]] = dot(table, arrived).astype(BF)
            contexts[h, 0] = spread(ctxg, (h,), ORDERS[h], 0)

    def context_on(step):
        for h in range(3):
            contexts[h, step - 1].wait_recv()
            contexts[h, step] = spread(ctxg, (h,), ORDERS[h], step)

    parts, hiddens, cores, ys, zs = {}, {}, {}, {}, {}

    def product(j):
        d = STEPS[j]
        zc = (z + 4 - d) % 4
        for copy in sib if d == 0 else [passed[d]]:
            copy.wait_recv()
        normalize(zc)
        rows = xn[...]
        for g in range(3):
            land(loads[2 * g:2 * g + 2])
            for t in range(0, 2 * third, wide_tile):
                value = dot(rows, wgu[:, 2 * g * third + t:2 * g * third + t + wide_tile])
                pb[j, g, :, :, :, :, t:t + wide_tile] = value.astype(BF).reshape(2, 2, 2, 16, wide_tile)
            one = ORDERS[g][0]
            parts[j, g, 1] = send(
                pb.at[spot((j, g), DIMS, {one: 1 - place[one]})], r1.at[j, g], w, across[one]
            )

    def halved(j):
        for g in range(3):
            one, two, three = ORDERS[g]
            rest = DIMS.replace(one, "")
            parts[j, g, 1].wait_recv()
            there = {two: 1 - place[two]}
            t2[j, g] = (
                pb[spot((j, g), DIMS, {one: place[one], **there})].astype(F32)
                + r1[spot((j, g), rest, there)].astype(F32)
            ).astype(BF)
            parts[j, g, 2] = send(t2.at[j, g], r2.at[j, g], w, across[two])

    def piece(j, g, last):
        one, two, three = ORDERS[g]
        rest = DIMS.replace(one, "")
        fixed = {one: place[one], two: place[two], three: last}
        return (
            pb[spot((j, g), DIMS, fixed)].astype(F32)
            + r1[spot((j, g), rest, fixed)].astype(F32)
            + r2[j, g, last].astype(F32)
        )

    def quartered(j):
        for g in range(3):
            three = ORDERS[g][2]
            parts[j, g, 2].wait_recv()
            t3[j, g] = piece(j, g, 1 - place[three]).astype(BF)
            parts[j, g, 3] = send(t3.at[j, g], r3.at[j, g], w, across[three])

    def hidden(j):
        for g in range(3):
            three = ORDERS[g][2]
            parts[j, g, 3].wait_recv()
            value = piece(j, g, place[three]) + r3[j, g].astype(F32)
            gate, up = value[:, :third], value[:, third:]
            hid[j, g, place["a"], place["b"], place["y"]] = (gate / (1.0 + jnp.exp(-gate)) * up).astype(BF)
            hiddens[j, g, 0] = spread(hid, (j, g), ORDERS[g], 0)

    def hidden_on(j, step):
        for g in range(3):
            hiddens[j, g, step - 1].wait_recv()
            hiddens[j, g, step] = spread(hid, (j, g), ORDERS[g], step)

    def result(j):
        zc = (z + 4 - STEPS[j]) % 4
        land(loads[7:9])
        for h in range(3):
            if contexts.get((h, 2)) is not None:
                contexts.pop((h, 2)).wait_recv()
        for g in range(3):
            hiddens[j, g, 2].wait_recv()
        rows = jnp.concatenate([hid[j, g].reshape(128, third) for g in range(3)], axis=1)
        cb_, cy = zc % 2, zc // 2
        heads = jnp.concatenate([
            jnp.concatenate([ctxg[h, cb_, cb_, cy], ctxg[h, 1 - cb_, cb_, cy]], axis=0) for h in range(3)
        ], axis=1)
        for t in range(0, wd.shape[1], wide_tile):
            cols = slice(t, t + wide_tile)
            value = (dot(rows, wd[:, cols]) + dot(heads, wo[:, cols])).reshape(2, 2, 32, wide_tile)
            acc[j, :, :, cols] = jnp.where(c == 0, value[:, 0], value[:, 1])
            cs[j, :, :, cols] = jnp.where(c == 0, value[:, 1], value[:, 0]).astype(BF)
        cores[j] = send(cs.at[j], rc.at[j], sw, n)

    def core_sum(j):
        d = STEPS[j]
        cores[j].wait_recv()
        sy[j] = (acc[j, 1 - yh] + rc[j, 1 - yh].astype(F32)).astype(BF)
        ys[j] = send(sy.at[j], ry.at[j], pw, n)
        acc[j, yh] += rc[j, yh].astype(F32)

    def y_sum(j):
        d = STEPS[j]
        ys[j].wait_recv()
        value = acc[j, yh] + ry[j].astype(F32)
        if d == 0:
            ysum[...] = value
        else:
            se[j] = value.astype(BF)
            zs[4 - d] = send(se.at[j], rz.at[4 - d], z_at(4 - d), n)

    turn(qs, qv, 1)
    statistics()
    turn(qs, qv, 2)
    gather(1)
    mates()
    turn(qs, qv, 3)
    gather(2)
    product(3)
    onward(3)
    gather(3)
    turn(qs, qv, 4)
    queries_in()
    onward(1)
    attend(0)
    attend(1)
    attend(2)
    attend(3)
    context_out()
    halved(3)
    gather(4)
    turn(csd, crv, 1)
    product(0)
    onward(2)
    product(1)
    turn(csd, crv, 2)
    product(2)
    halved(0)
    quartered(3)
    turn(csd, crv, 3)
    halved(1)
    halved(2)
    quartered(0)
    turn(csd, crv, 4)
    context_in()
    quartered(1)
    hidden(3)
    quartered(2)
    hidden(0)
    context_on(1)
    hidden(1)
    hidden_on(3, 1)
    hidden_on(0, 1)
    hidden(2)
    context_on(2)
    hidden_on(1, 1)
    hidden_on(0, 2)
    hidden_on(2, 1)
    hidden_on(1, 2)
    result(0)
    hidden_on(3, 2)
    hidden_on(2, 2)
    result(1)
    core_sum(0)
    core_sum(1)
    result(2)
    result(3)
    core_sum(2)
    y_sum(0)
    y_sum(1)
    core_sum(3)
    y_sum(2)
    drain()
    y_sum(3)

    value = ysum[...]
    for e in (3, 1, 2):
        zs[e].wait_recv()
        value += rz[e].astype(F32)
    out[...] = value.astype(BF)
    drain()


def local(residual_in, query, cache, lengths, gate_weight, up_weight, down_weight, out_weight):
    rows, width = residual_in.shape
    half = gate_weight.shape[1]
    cols = query.shape[1]
    places = cache.shape[2]
    vmem = pl.BlockSpec(memory_space=pltpu.VMEM)
    hbm = pl.BlockSpec(memory_space=pl.ANY)
    copies = 176
    return pl.pallas_call(
        kernel,
        out_shape=jax.ShapeDtypeStruct((rows, width), BF),
        in_specs=[vmem, vmem, pl.BlockSpec(memory_space=pltpu.SMEM), hbm, hbm, hbm, hbm, hbm],
        out_specs=vmem,
        scratch_shapes=[
            pltpu.VMEM((width, 2 * half), BF),
            pltpu.VMEM((half, width), BF),
            pltpu.VMEM((cols, width), BF),
            pltpu.VMEM((4, places, 2 * HEAD), BF),
            pltpu.VMEM((4, 2, 2, 32, width), BF),
            pltpu.VMEM((128, width), BF),
            pltpu.VMEM((8, 32, 128), F32),
            pltpu.VMEM((2, 2, 2, 2, 8, 128), F32),
            pltpu.VMEM((4, 3, 2, 2, 2, 16, 2 * half // 3), BF),
            pltpu.VMEM((4, 3, 2, 2, 16, 2 * half // 3), BF),
            pltpu.VMEM((4, 3, 2, 16, 2 * half // 3), BF),
            pltpu.VMEM((4, 3, 2, 16, 2 * half // 3), BF),
            pltpu.VMEM((4, 3, 16, 2 * half // 3), BF),
            pltpu.VMEM((4, 3, 16, 2 * half // 3), BF),
            pltpu.VMEM((4, 3, 2, 2, 2, 16, half // 3), BF),
            pltpu.VMEM((3, 2, 2, 2, 64, HEAD), BF),
            pltpu.VMEM((4, 2, 32, width), F32),
            pltpu.VMEM((4, 2, 32, width), BF),
            pltpu.VMEM((4, 2, 32, width), BF),
            pltpu.VMEM((4, 32, width), BF),
            pltpu.VMEM((4, 32, width), BF),
            pltpu.VMEM((32, width), F32),
            pltpu.VMEM((4, 32, width), BF),
            pltpu.VMEM((4, 32, width), BF),
            pltpu.VMEM((2, 2, 2, 2, 16, HEAD), BF),
            pltpu.VMEM((4, 2, 2, 2, 16, HEAD), BF),
            pltpu.VMEM((192, HEAD), BF),
            pltpu.VMEM((192, HEAD), BF),
            pltpu.VMEM((2, 2, 2, 2, 16, HEAD), BF),
            pltpu.VMEM((4, 2, 2, 2, 16, HEAD), BF),
            pltpu.SemaphoreType.DMA((9,)),
            pltpu.SemaphoreType.DMA((copies,)),
            pltpu.SemaphoreType.DMA((copies,)),
        ],
        compiler_params=pltpu.CompilerParams(
            collective_id=0, has_side_effects=True, vmem_limit_bytes=58 << 20
        ),
        name="layer",
    )(residual_in, query, lengths, cache, gate_weight, up_weight, down_weight, out_weight)


def solution(mesh):
    return jax.shard_map(
        local,
        mesh=mesh,
        in_specs=(
            P("wide", "narrow"),
            P("narrow", "wide"),
            P("narrow", "wide", None, None),
            P("narrow", "wide"),
            P("narrow", "wide"),
            P("narrow", "wide"),
            P("wide", "narrow"),
            P("wide", "narrow"),
        ),
        out_specs=P("wide", "narrow"),
        check_vma=False,
    )
```

```python
import jax
import jax.numpy as jnp
from jax import lax
from jax.experimental import pallas as pl
from jax.experimental.pallas import tpu as pltpu
from jax.sharding import PartitionSpec as P

HEADS = 48
HEAD = 256
MESH = pl.DeviceIdType.MESH
BF = jnp.bfloat16
F32 = jnp.float32
STEPS = (1, 3, 2, 0)
Z_FIRST = (1, 3)
DIMS = "aby"
ORDERS = ("aby", "bya", "yab")
WIDE = "abhc"
TURNS = "chab"


def whole(p):
    return 4 * (2 * ((p >> 2) & 1) + ((p >> 3) ^ ((p >> 2) & 1))) + (p & 3)


def dot(a, b):
    return jnp.dot(a, b, preferred_element_type=F32)


def pick(rows, cols, rule):
    i = lax.broadcasted_iota(jnp.int32, (rows, cols), 0)
    k = lax.broadcasted_iota(jnp.int32, (rows, cols), 1)
    return jnp.where(rule(i, k), 1.0, 0.0).astype(BF)


def kernel(
    res, query, lengths, cache_hbm, wg_hbm, wu_hbm, wd_hbm, wo_hbm, out,
    wgu, wd, wo, cache, xg, xn, st, sg, pb, r1, t2, r2, t3, r3, hid, ctxg, acc, cs, rc, sy, ry, ysum, se, rz, sz, rzz,
    qs, qv, qh, cb, csd, crv, lsem, ssem, rsem,
):
    w = lax.axis_index("wide")
    n = lax.axis_index("narrow")
    z, yh, c = w // 4, (w // 2) % 2, w % 2
    yl, x = n // 4, n % 4
    width = res.shape[1] * 8
    half = wg_hbm.shape[1]
    third = half // 3
    wide_tile = 256
    taken = [0]
    pending = []

    place = {"a": ((x + 1) % 4) // 2, "b": x // 2, "y": yl}
    across = {"a": yl * 4 + x + 1 - 2 * (x % 2), "b": yl * 4 + 3 - x, "y": (1 - yl) * 4 + x}

    pw = z * 4 + (1 - yh) * 2 + c
    sw = z * 4 + yh * 2 + (1 - c)
    wplace = {"a": ((z + 1) % 4) // 2, "b": z // 2, "h": yh, "c": c}
    wacross = {"a": (z + 1 - 2 * (z % 2)) * 4 + yh * 2 + c, "b": (3 - z) * 4 + yh * 2 + c, "h": pw, "c": sw}

    def spot(lead, dims, fixed):
        return tuple(lead) + tuple(fixed.get(d, slice(None)) for d in dims)

    def near(k):
        return ((yl + k // 4) % 2) * 4 + (x + k % 4) % 4

    def z_at(d):
        return ((z + d) % 4) * 4 + yh * 2 + c

    def send(src, dst, wt, nt):
        i = taken[0]
        taken[0] += 1
        copy = pltpu.make_async_remote_copy(
            src_ref=src, dst_ref=dst, send_sem=ssem.at[i], recv_sem=rsem.at[i],
            device_id=(wt, nt), device_id_type=MESH,
        )
        copy.start()
        pending.append(copy)
        return copy

    def drain(keep=0):
        done = len(pending) - keep
        for copy in pending[:done]:
            copy.wait_send()
        del pending[:done]

    loads = []

    landed = set()

    def load(src, dst):
        copy = pltpu.make_async_copy(src, dst, lsem.at[len(loads)])
        copy.start()
        loads.append(copy)

    def land(copies):
        for copy in copies:
            if id(copy) not in landed:
                landed.add(id(copy))
                copy.wait()

    for g in range(3):
        load(wg_hbm.at[:, pl.ds(g * third, third)], wgu.at[:, pl.ds(2 * g * third, third)])
        load(wu_hbm.at[:, pl.ds(g * third, third)], wgu.at[:, pl.ds((2 * g + 1) * third, third)])

    barrier = pltpu.get_barrier_semaphore()
    for k in range(1, 8):
        pl.semaphore_signal(barrier, inc=1, device_id=(w, near(k)), device_id_type=MESH)
    for peer in (sw, pw, z_at(1), z_at(3), z_at(2)):
        pl.semaphore_signal(barrier, inc=1, device_id=(peer, n), device_id_type=MESH)

    xg[z, yh, c] = res[...]

    rows_f = res[...].astype(F32)
    total = jnp.sum(rows_f, axis=1, keepdims=True)
    square = jnp.sum(rows_f * rows_f, axis=1, keepdims=True)
    lane = lax.broadcasted_iota(jnp.int32, (32, 128), 1)
    mine = jnp.where(lane < 64, total, square)
    st[0] = mine
    pl.semaphore_wait(barrier, 12)

    turns = {}

    def turn(held, landing, step):
        if step > 0:
            turns[step - 1].wait_recv()
            turns[step - 1].wait_send()
            pending[:] = [copy for copy in pending if copy is not turns[step - 1]]
            d = TURNS[step - 1]
            held[spot((), WIDE, {d: 1 - wplace[d]})] = landing[step - 1]
        if step < 4:
            d = TURNS[step]
            turns[step] = send(held.at[spot((), WIDE, {d: 1 - wplace[d]})], landing.at[step], wacross[d], n)


    def rows_at(zz, yy):
        return xg.at[zz, yy, c]

    mate = send(rows_at(z, yh), rows_at(z, yh), pw, n)
    first = {d: send(rows_at(z, yh), rows_at(z, yh), z_at(d), n) for d in (1, 3)}
    stats = [send(st.at[0], st.at[k], w, near(k)) for k in range(1, 8)]
    sib = [send(rows_at(z, yh), rows_at(z, yh), sw, n)]
    second, passed, gathers = {}, {}, {}
    moved = jnp.zeros((256, HEAD), F32)
    for h in range(3):
        table = pick(256, 64, lambda i, k: (whole(i >> 4) == (k >> 2)) & ((i & 15) == 4 * h + (k & 3)))
        moved += dot(table, query[:, h * HEAD:(h + 1) * HEAD])
    qs[...] = moved.astype(BF).reshape(2, 2, 2, 2, 16, HEAD)
    turn(qs, qv, 0)
    load(cache_hbm.at[0], cache)

    def gather(step):
        if step > 0:
            gathers[step - 1].wait_recv()
        if step < 4:
            d = TURNS[step]
            region = sg.at[spot((), WIDE, {e: wplace[e] for e in TURNS[step:]})]
            gathers[step] = send(region, region, wacross[d], n)

    def statistics():
        sums = mine
        for k, copy in enumerate(stats):
            copy.wait_recv()
            sums += st[k + 1]
        mean = sums[:, 0:1] / width
        variance = sums[:, 64:65] / width - mean * mean
        scale = lax.rsqrt(variance + 1e-06)
        row = lax.broadcasted_iota(jnp.int32, (32, 128), 0)
        line = jnp.sum(
            jnp.where(lane == row, mean, 0.0) + jnp.where(lane == row + 32, scale, 0.0), axis=0, keepdims=True
        )
        sg[wplace["a"], wplace["b"], yh, c] = jnp.broadcast_to(line, (8, 128))
        gather(0)

    def normalize(zc):
        row = lax.broadcasted_iota(jnp.int32, (32, 128), 0)
        for h in range(2):
            for k in range(2):
                line = sg[((zc + 1) % 4) // 2, zc // 2, h, k][0:1, :]
                mean = jnp.sum(jnp.where(lane == row, line, 0.0), axis=1, keepdims=True)
                scale = jnp.sum(jnp.where(lane == row + 32, line, 0.0), axis=1, keepdims=True)
                at = (2 * h + k) * 32
                xn[at:at + 32, :] = ((xg[zc, h, k].astype(F32) - mean) * scale).astype(BF)

    def mates():
        mate.wait_recv()
        for d in (1, 3):
            second[d] = send(rows_at(z, 1 - yh), rows_at(z, 1 - yh), z_at(d), n)
        sib.append(send(rows_at(z, 1 - yh), rows_at(z, 1 - yh), sw, n))
        load(wo_hbm, wo)
        load(wd_hbm, wd)

    def onward(d):
        zc = (z + 4 - d) % 4
        first[d].wait_recv()
        if d == 1:
            first[2] = send(rows_at(zc, yh), rows_at(zc, yh), z_at(1), n)
        second[d].wait_recv()
        if d == 3:
            second[2] = send(rows_at(zc, 1 - yh), rows_at(zc, 1 - yh), z_at(3), n)
        passed[d] = send(xg.at[zc, :, c], xg.at[zc, :, c], sw, n)

    def queries_in():
        table = pick(
            192, 256,
            lambda i, k: (i == (k & 3) * 48 + whole(k >> 4) * 3 + ((k >> 2) & 3)) & (((k >> 2) & 3) < 3),
        )
        qh[...] = dot(table, qs[...].reshape(256, HEAD)).astype(BF)
        land(loads[6:7])

    def attend(r):
        scores = lax.dot_general(
            qh[r * 48:(r + 1) * 48, :], cache[r, :, 0:HEAD], (((1,), (1,)), ((), ())),
            preferred_element_type=F32,
        ) * (1.0 / 16.0)
        at = lax.broadcasted_iota(jnp.int32, scores.shape, 1)
        scores = jnp.where(at < lengths[0, r], scores, -jnp.inf)
        top = jnp.max(scores, axis=1, keepdims=True)
        weights = jnp.exp(scores - top)
        probs = (weights / jnp.sum(weights, axis=1, keepdims=True)).astype(BF)
        cb[r * 48:(r + 1) * 48, :] = dot(probs, cache[r, :, HEAD:2 * HEAD]).astype(BF)

    contexts = {}

    def context_out():
        table = pick(
            256, 192,
            lambda k, i: (i == (k & 3) * 48 + whole(k >> 4) * 3 + ((k >> 2) & 3)) & (((k >> 2) & 3) < 3),
        )
        csd[...] = dot(table, cb[...]).astype(BF).reshape(2, 2, 2, 2, 16, HEAD)
        turn(csd, crv, 0)

    def spread(ref, lead, order, step):
        fixed = {d: place[d] for d in order[:3 - step]}
        region = ref.at[spot(lead, DIMS, fixed)]
        return send(region, region, w, across[order[2 - step]])

    def context_in():
        arrived = csd[...].reshape(256, HEAD)
        for h in range(3):
            table = pick(64, 256, lambda i, k: (whole(k >> 4) == (i >> 2)) & ((k & 15) == 4 * h + (i & 3)))
            ctxg[h, place["a"], place["b"], place["y"]] = dot(table, arrived).astype(BF)
            contexts[h, 0] = spread(ctxg, (h,), ORDERS[h], 0)

    def context_on(step):
        for h in range(3):
            contexts[h, step - 1].wait_recv()
            contexts[h, step] = spread(ctxg, (h,), ORDERS[h], step)

    parts, hiddens, cores, ys, zs = {}, {}, {}, {}, {}

    def product(j):
        d = STEPS[j]
        zc = (z + 4 - d) % 4
        for copy in sib if d == 0 else [passed[d]]:
            copy.wait_recv()
        normalize(zc)
        rows = xn[...]
        for g in range(3):
            land(loads[2 * g:2 * g + 2])
            for t in range(0, 2 * third, wide_tile):
                value = dot(rows, wgu[:, 2 * g * third + t:2 * g * third + t + wide_tile])
                pb[j, g, :, :, :, :, t:t + wide_tile] = value.astype(BF).reshape(2, 2, 2, 16, wide_tile)
            one = ORDERS[g][0]
            parts[j, g, 1] = send(
                pb.at[spot((j, g), DIMS, {one: 1 - place[one]})], r1.at[j, g], w, across[one]
            )

    def halved(j):
        for g in range(3):
            one, two, three = ORDERS[g]
            rest = DIMS.replace(one, "")
            parts[j, g, 1].wait_recv()
            there = {two: 1 - place[two]}
            t2[j, g] = (
                pb[spot((j, g), DIMS, {one: place[one], **there})].astype(F32)
                + r1[spot((j, g), rest, there)].astype(F32)
            ).astype(BF)
            parts[j, g, 2] = send(t2.at[j, g], r2.at[j, g], w, across[two])

    def piece(j, g, last):
        one, two, three = ORDERS[g]
        rest = DIMS.replace(one, "")
        fixed = {one: place[one], two: place[two], three: last}
        return (
            pb[spot((j, g), DIMS, fixed)].astype(F32)
            + r1[spot((j, g), rest, fixed)].astype(F32)
            + r2[j, g, last].astype(F32)
        )

    def quartered(j):
        for g in range(3):
            three = ORDERS[g][2]
            parts[j, g, 2].wait_recv()
            t3[j, g] = piece(j, g, 1 - place[three]).astype(BF)
            parts[j, g, 3] = send(t3.at[j, g], r3.at[j, g], w, across[three])

    def hidden(j):
        for g in range(3):
            three = ORDERS[g][2]
            parts[j, g, 3].wait_recv()
            value = piece(j, g, place[three]) + r3[j, g].astype(F32)
            gate, up = value[:, :third], value[:, third:]
            hid[j, g, place["a"], place["b"], place["y"]] = (gate / (1.0 + jnp.exp(-gate)) * up).astype(BF)
            hiddens[j, g, 0] = spread(hid, (j, g), ORDERS[g], 0)

    def hidden_on(j, step):
        for g in range(3):
            hiddens[j, g, step - 1].wait_recv()
            hiddens[j, g, step] = spread(hid, (j, g), ORDERS[g], step)

    def result(j):
        zc = (z + 4 - STEPS[j]) % 4
        land(loads[7:9])
        for h in range(3):
            if contexts.get((h, 2)) is not None:
                contexts.pop((h, 2)).wait_recv()
        for g in range(3):
            hiddens[j, g, 2].wait_recv()
        rows = jnp.concatenate([hid[j, g].reshape(128, third) for g in range(3)], axis=1)
        cb_, cy = zc % 2, zc // 2
        heads = jnp.concatenate([
            jnp.concatenate([ctxg[h, cb_, cb_, cy], ctxg[h, 1 - cb_, cb_, cy]], axis=0) for h in range(3)
        ], axis=1)
        for t in range(0, wd.shape[1], wide_tile):
            cols = slice(t, t + wide_tile)
            value = (dot(rows, wd[:, cols]) + dot(heads, wo[:, cols])).reshape(2, 2, 32, wide_tile)
            acc[j, :, :, cols] = jnp.where(c == 0, value[:, 0], value[:, 1])
            cs[j, :, :, cols] = jnp.where(c == 0, value[:, 1], value[:, 0]).astype(BF)
        cores[j] = send(cs.at[j], rc.at[j], sw, n)

    def core_sum(j):
        d = STEPS[j]
        cores[j].wait_recv()
        if d in Z_FIRST:
            sz[j] = (acc[j] + rc[j].astype(F32)).astype(BF)
            zs[4 - d] = send(sz.at[j], rzz.at[4 - d], z_at(4 - d), n)
            return
        there = acc[j, 1 - yh] + rc[j, 1 - yh].astype(F32)
        here = acc[j, yh] + rc[j, yh].astype(F32)
        if d == 0:
            for e in Z_FIRST:
                zs[4 - e].wait_recv()
                there += rzz[4 - e, 1 - yh].astype(F32)
                here += rzz[4 - e, yh].astype(F32)
        sy[j] = there.astype(BF)
        ys[j] = send(sy.at[j], ry.at[j], pw, n)
        acc[j, yh] = here

    def y_sum(j):
        d = STEPS[j]
        ys[j].wait_recv()
        value = acc[j, yh] + ry[j].astype(F32)
        if d == 0:
            ysum[...] = value
        else:
            se[j] = value.astype(BF)
            zs[4 - d] = send(se.at[j], rz.at[4 - d], z_at(4 - d), n)

    turn(qs, qv, 1)
    statistics()
    turn(qs, qv, 2)
    mates()
    gather(1)
    turn(qs, qv, 3)
    gather(2)
    product(3)
    onward(3)
    gather(3)
    onward(1)
    turn(qs, qv, 4)
    queries_in()
    attend(0)
    attend(1)
    attend(2)
    attend(3)
    context_out()
    halved(3)
    gather(4)
    turn(csd, crv, 1)
    product(0)
    onward(2)
    product(1)
    turn(csd, crv, 2)
    product(2)
    halved(0)
    quartered(3)
    turn(csd, crv, 3)
    halved(1)
    halved(2)
    quartered(0)
    turn(csd, crv, 4)
    context_in()
    quartered(1)
    quartered(2)
    hidden(0)
    context_on(1)
    hidden(1)
    hidden(3)
    hidden_on(0, 1)
    hidden(2)
    hidden_on(1, 1)
    context_on(2)
    hidden_on(2, 1)
    hidden_on(0, 2)
    hidden_on(3, 1)
    hidden_on(1, 2)
    hidden_on(2, 2)
    result(0)
    result(1)
    result(2)
    core_sum(0)
    core_sum(1)
    hidden_on(3, 2)
    core_sum(2)
    result(3)
    y_sum(2)
    drain(10)
    core_sum(3)
    y_sum(3)

    value = ysum[...]
    for d in (1, 3, 2):
        if d not in Z_FIRST:
            zs[4 - d].wait_recv()
            value += rz[4 - d].astype(F32)
    out[...] = value.astype(BF)
    drain()


def local(residual_in, query, cache, lengths, gate_weight, up_weight, down_weight, out_weight):
    rows, width = residual_in.shape
    half = gate_weight.shape[1]
    cols = query.shape[1]
    places = cache.shape[2]
    vmem = pl.BlockSpec(memory_space=pltpu.VMEM)
    hbm = pl.BlockSpec(memory_space=pl.ANY)
    copies = 176
    return pl.pallas_call(
        kernel,
        out_shape=jax.ShapeDtypeStruct((rows, width), BF),
        in_specs=[vmem, vmem, pl.BlockSpec(memory_space=pltpu.SMEM), hbm, hbm, hbm, hbm, hbm],
        out_specs=vmem,
        scratch_shapes=[
            pltpu.VMEM((width, 2 * half), BF),
            pltpu.VMEM((half, width), BF),
            pltpu.VMEM((cols, width), BF),
            pltpu.VMEM((4, places, 2 * HEAD), BF),
            pltpu.VMEM((4, 2, 2, 32, width), BF),
            pltpu.VMEM((128, width), BF),
            pltpu.VMEM((8, 32, 128), F32),
            pltpu.VMEM((2, 2, 2, 2, 8, 128), F32),
            pltpu.VMEM((4, 3, 2, 2, 2, 16, 2 * half // 3), BF),
            pltpu.VMEM((4, 3, 2, 2, 16, 2 * half // 3), BF),
            pltpu.VMEM((4, 3, 2, 16, 2 * half // 3), BF),
            pltpu.VMEM((4, 3, 2, 16, 2 * half // 3), BF),
            pltpu.VMEM((4, 3, 16, 2 * half // 3), BF),
            pltpu.VMEM((4, 3, 16, 2 * half // 3), BF),
            pltpu.VMEM((4, 3, 2, 2, 2, 16, half // 3), BF),
            pltpu.VMEM((3, 2, 2, 2, 64, HEAD), BF),
            pltpu.VMEM((4, 2, 32, width), F32),
            pltpu.VMEM((4, 2, 32, width), BF),
            pltpu.VMEM((4, 2, 32, width), BF),
            pltpu.VMEM((4, 32, width), BF),
            pltpu.VMEM((4, 32, width), BF),
            pltpu.VMEM((32, width), F32),
            pltpu.VMEM((4, 32, width), BF),
            pltpu.VMEM((4, 32, width), BF),
            pltpu.VMEM((4, 2, 32, width), BF),
            pltpu.VMEM((4, 2, 32, width), BF),
            pltpu.VMEM((2, 2, 2, 2, 16, HEAD), BF),
            pltpu.VMEM((4, 2, 2, 2, 16, HEAD), BF),
            pltpu.VMEM((192, HEAD), BF),
            pltpu.VMEM((192, HEAD), BF),
            pltpu.VMEM((2, 2, 2, 2, 16, HEAD), BF),
            pltpu.VMEM((4, 2, 2, 2, 16, HEAD), BF),
            pltpu.SemaphoreType.DMA((9,)),
            pltpu.SemaphoreType.DMA((copies,)),
            pltpu.SemaphoreType.DMA((copies,)),
        ],
        compiler_params=pltpu.CompilerParams(
            collective_id=0, has_side_effects=True, vmem_limit_bytes=58 << 20
        ),
        name="layer",
    )(residual_in, query, lengths, cache, gate_weight, up_weight, down_weight, out_weight)


def solution(mesh):
    return jax.shard_map(
        local,
        mesh=mesh,
        in_specs=(
            P("wide", "narrow"),
            P("narrow", "wide"),
            P("narrow", "wide", None, None),
            P("narrow", "wide"),
            P("narrow", "wide"),
            P("narrow", "wide"),
            P("wide", "narrow"),
            P("wide", "narrow"),
        ),
        out_specs=P("wide", "narrow"),
        check_vma=False,
    )
```
